32 devices in a mesh: section: 8 (over z, core), dp: 4 (over y, x).
Axes of the slice: x: 2, y: 2, z: 4, core: 2. Of those that a mesh axis runs over, the one named last changes fastest.
Arguments:
- stream_in: bfloat16 [8, 2, 256, 6144], P('section', None, 'dp'), may hold values from -600 to 600
- gain: bfloat16 [8, 6144], P('section'), may hold values from 0.5 to 1.5
- kv_weight: bfloat16 [8, 6144, 1024], P('section'), may hold values from -21 to 21
- pattern: int32 [2, 2, 2], replicated, may hold values from 0 to 1, as said below
- top_grad: bfloat16 [2, 256, 6144], P(None, 'dp'), may hold values from -6 to 6
Outputs:
- stream_grads: bfloat16 [8, 2, 256, 6144], P('section', None, 'dp')
- weight_grads: bfloat16 [8, 6144, 1024], P('section', 'dp')
The draws below stay inside these ranges and needn't reach their ends.
Inputs may be any that keep to these rules, and one draw needn't show every extreme that they name: `pattern`: entries are 0 or 1; tiles above the diagonal are 0 and diagonal tiles are 1.
All inputs are finite; a program needn't handle non-finite values.
Results may differ from the reference program's by a relative error of at most 0.03.
The reference program's roundings to bfloat16 on the way count: a program that leaves them out, or rounds other values in their place, can miss the bound.
Values may be sent and summed in bfloat16 or wider, within the bound.
A program may use at most 128 MiB of HBM per device.

```python
import math
import jax
import jax.numpy as jnp
from jax import lax

H = 48
DH = 128
KVH = 4
D = 6144
TILE = 128
TOK = 64
MICRO = 2
SECTIONS = 8
SEQ = 256
NT = 2
N_SECTION = 8
N_DP = 4


def draw_stream_in(key, part):
    key = jax.random.fold_in(key, 11)
    scale_key = jax.random.fold_in(key, 0)
    base_key = jax.random.fold_in(key, 2)
    column_scale = jnp.exp(jax.random.uniform(scale_key, (SECTIONS, 1, 1, D)) * math.log(10.0))
    values = jax.random.truncated_normal(base_key, -6.0, 6.0, (SECTIONS, MICRO, SEQ, D)) * column_scale
    return values.astype(jnp.bfloat16)


def draw_kv_weight(key, part):
    key = jax.random.fold_in(key, 23)
    values = jax.random.truncated_normal(key, -6.0, 6.0, (SECTIONS, D, 2 * KVH * DH)) / math.sqrt(D)
    return values.astype(jnp.bfloat16)


def draw_pattern(key, part):
    key = jax.random.fold_in(key, 37)
    random_bits = jax.random.randint(key, (MICRO, NT, NT), 0, 2)
    lower = jnp.tril(random_bits, -1)
    return (lower + jnp.eye(NT, dtype=jnp.int32)[None]).astype(jnp.int32)


def block_levels(key, extent, cuts, low, top_value):
    factor_of = 1.0
    for position, shards_of in cuts:
        draws = jax.random.uniform(jax.random.fold_in(jax.random.fold_in(key, 6), position), (shards_of,), jnp.float32, low / len(cuts), top_value / len(cuts))
        factor_of = factor_of * jnp.repeat(jnp.exp(draws), extent[position] // shards_of).reshape((-1,) + (1,) * (len(extent) - 1 - position))
    return factor_of


def gaussian(rng, extent, scale, most, cuts=(), kind=jnp.bfloat16):
    values = scale * jax.random.normal(rng, extent, jnp.float32)
    if cuts:
        values = values * block_levels(rng, extent, cuts, -0.22, 0.18)
    return jnp.clip(values, -most, most).astype(kind)


def setup_inputs(seed: int = 0) -> dict:
    splits = jax.random.split(jax.random.key(seed), 6)
    return {
        "stream_in": draw_stream_in(jax.random.fold_in(splits[5], 71), 0),
        "gain": jnp.clip(1.0 + 0.1 * jax.random.normal(splits[1], (SECTIONS, D), jnp.float32), 0.5, 1.5).astype(jnp.bfloat16),
        "kv_weight": draw_kv_weight(jax.random.fold_in(splits[5], 71), 0),
        "pattern": draw_pattern(jax.random.fold_in(splits[5], 71), 0),
        "top_grad": gaussian(splits[4], (MICRO, SEQ, D), 1.0, 6.0, ((1, 4),)),
    }


def block_sum(weights, rows):
    heads = weights.shape[0]
    reshaped_tensor = weights.reshape(heads, N_DP, TOK, SEQ)
    block_row_groups = rows.reshape(N_DP, TOK, heads, DH)
    split_pieces = jnp.einsum('rzfs,zfrw->zsw', reshaped_tensor, block_row_groups)
    return lax.optimization_barrier(jnp.sum(split_pieces.astype(jnp.bfloat16).astype(jnp.float32), axis=0))

def section_backward(stream, gain_row, weight_matrix, tile_mask, upstream):
    group_size = H // KVH
    kv_width = KVH * DH
    score_scale = 1.0 / math.sqrt(DH)
    stream_f = stream.astype(jnp.float32)
    inverse_rms = lax.rsqrt(lax.optimization_barrier(jnp.mean(stream_f * stream_f, axis=-1, keepdims=True)) + 1e-05)
    gain_f = gain_row.astype(jnp.float32)
    normalized_rows = (stream_f * inverse_rms * gain_f).astype(jnp.bfloat16)
    keyval = jnp.dot(normalized_rows, weight_matrix, preferred_element_type=jnp.float32).astype(jnp.bfloat16)
    tiles_full = jnp.repeat(jnp.repeat(tile_mask, TILE, axis=0), TILE, axis=1) > 0
    positions = jnp.arange(SEQ)
    allowed = tiles_full & (positions[None, :] <= positions[:, None])
    upstream_f = upstream.astype(jnp.float32)
    query_parts = []
    key_parts = []
    value_parts = []
    for head_group in range(KVH):
        low = head_group * group_size * DH
        high = low + group_size * DH
        queries = normalized_rows[:, low:high].reshape(SEQ, group_size, DH).astype(jnp.float32)
        key_rows = keyval[:, head_group * DH:(head_group + 1) * DH].astype(jnp.float32)
        value_rows = keyval[:, kv_width + head_group * DH:kv_width + (head_group + 1) * DH].astype(jnp.float32)
        scores = jnp.einsum('qhd,kd->hqk', queries, key_rows) * score_scale
        scores = jnp.where(allowed[None], scores, -1e+30)
        row_peak = lax.optimization_barrier(jnp.max(scores, axis=-1, keepdims=True))
        expo = jnp.exp(scores - row_peak)
        soft_weights = expo / lax.optimization_barrier(jnp.sum(expo, axis=-1, keepdims=True))
        soft_rounded = soft_weights.astype(jnp.bfloat16).astype(jnp.float32)
        attn_out = jnp.einsum('hqk,kd->qhd', soft_rounded, value_rows).astype(jnp.bfloat16).astype(jnp.float32)
        heads_up = upstream_f[:, low:high].reshape(SEQ, group_size, DH)
        delta = lax.optimization_barrier(jnp.sum(heads_up * attn_out, axis=-1))
        value_parts.append(block_sum(soft_rounded, heads_up))
        dprobs = jnp.einsum('qhd,kd->hqk', heads_up, value_rows)
        dscores = (soft_weights * (dprobs - delta.T[:, :, None]) * score_scale).astype(jnp.bfloat16).astype(jnp.float32)
        query_parts.append(jnp.einsum('hqk,kd->qhd', dscores, key_rows).reshape(SEQ, group_size * DH))
        key_parts.append(block_sum(dscores, queries))
    dkeyval = jnp.concatenate(key_parts + value_parts, axis=1).astype(jnp.bfloat16)
    normalized_input_grad = jnp.concatenate(query_parts, axis=1) + jnp.dot(dkeyval, weight_matrix.T, preferred_element_type=jnp.float32)
    scaled = gain_f * normalized_input_grad
    grad_in = upstream_f + inverse_rms * scaled - stream_f * inverse_rms ** 3 * lax.optimization_barrier(jnp.mean(stream_f * scaled, axis=-1, keepdims=True))
    weight_term = jnp.dot(normalized_rows.T, dkeyval, preferred_element_type=jnp.float32)
    return (grad_in.astype(jnp.bfloat16), weight_term)

def reference(stream_in, gain, kv_weight, pattern, top_grad):
    incoming = [top_grad[slot] for slot in range(MICRO)]
    per_section_gradient = [None] * N_SECTION
    section_weights = [None] * N_SECTION
    for section_number in reversed(range(N_SECTION)):
        outgoing = []
        total = jnp.zeros((D, 2 * KVH * DH), jnp.float32)
        for slot in range(MICRO):
            grad_in, weight_term = section_backward(stream_in[section_number, slot], gain[section_number], kv_weight[section_number], pattern[slot], incoming[slot])
            outgoing.append(grad_in)
            total = total + weight_term
        incoming = outgoing
        per_section_gradient[section_number] = jnp.stack(outgoing)
        section_weights[section_number] = total.astype(jnp.bfloat16)
    return (jnp.stack(per_section_gradient), jnp.stack(section_weights))
```

```python
import functools
import math

import jax
import jax.numpy as jnp
from jax import lax
from jax.experimental import pallas as pl
from jax.experimental.pallas import tpu as pltpu
from jax.sharding import PartitionSpec as P

H = 48
DH = 128
KVH = 4
TILE = 128
GROUP = H // KVH
SCALE = 1.0 / math.sqrt(DH)
MESH = pl.DeviceIdType.MESH
NT_DIMS = (((1,), (1,)), ((), ()))
TN_DIMS = (((0,), (0,)), ((), ()))


def relay(
    sections, ranks, micros, tokens,
    top, stream, normed, inverse, gain, weight, keyval, probs, attn, keyval_raw, normed_t,
    grads, wgrad,
    up, part, landed, dquery, total, dkv, dkv_all, mean,
    up_send, up_recv, part_send, part_recv, dkv_send, dkv_recv,
):
    sec = lax.axis_index("section")
    me = lax.axis_index("dp")
    width = GROUP * DH
    model = width * KVH

    barrier = pltpu.get_barrier_semaphore()
    for step in (1, sections - 1):
        pl.semaphore_signal(
            barrier, inc=1, device_id=(lax.rem(sec + step, sections), me), device_id_type=MESH
        )
    for step in range(1, ranks):
        pl.semaphore_signal(
            barrier, inc=1, device_id=(sec, lax.rem(me + step, ranks)), device_id_type=MESH
        )
    pl.semaphore_wait(barrier, 2 + ranks - 1)

    @pl.when(sec == sections - 1)
    def _():
        up[...] = top[...]

    def cols(g):
        return pl.ds(pl.multiple_of(g * width, 128), width)

    def up_copy(m, g):
        return pltpu.make_async_remote_copy(
            src_ref=grads.at[m, :, cols(g)],
            dst_ref=up.at[m, :, cols(g)],
            send_sem=up_send.at[m, g],
            recv_sem=up_recv.at[m, g],
            device_id=(lax.rem(sec + sections - 1, sections), me),
            device_id_type=MESH,
        )

    def part_copy(m, g, slot, peer):
        rows = pl.ds(pl.multiple_of(peer * tokens, tokens), tokens)
        return pltpu.make_async_remote_copy(
            src_ref=part.at[m, g, rows, :],
            dst_ref=landed.at[m, g, slot],
            send_sem=part_send.at[m, g, slot],
            recv_sem=part_recv.at[m, g, slot],
            device_id=(sec, peer),
            device_id_type=MESH,
        )

    def dkv_copy(m, step):
        return pltpu.make_async_remote_copy(
            src_ref=dkv.at[m],
            dst_ref=dkv_all.at[m, step],
            send_sem=dkv_send.at[m, step],
            recv_sem=dkv_recv.at[m, step],
            device_id=(sec, lax.rem(me + step + 1, ranks)),
            device_id_type=MESH,
        )

    def stacked(block):
        return jnp.concatenate([block[:, h * DH : (h + 1) * DH] for h in range(GROUP)], axis=0)

    def attend(m, g):
        @pl.when(sec < sections - 1)
        def _():
            up_copy(m, g).wait_recv()

        ups = stacked(up[m, :, cols(g)])
        queries = stacked(normed[m, :, cols(g)])
        keys = keyval[m, :, pl.ds(pl.multiple_of(g * DH, DH), DH)]
        values = keyval[m, :, pl.ds(pl.multiple_of((KVH + g) * DH, DH), DH)]
        delta = jnp.sum(
            ups.astype(jnp.float32) * attn[m, g].astype(jnp.float32), axis=-1, keepdims=True
        )
        soft = probs[m, g]
        part[m, g, :, DH:] = lax.dot_general(
            soft.astype(jnp.bfloat16), ups, TN_DIMS, preferred_element_type=jnp.float32
        ).astype(jnp.bfloat16)
        dprobs = lax.dot_general(ups, values, NT_DIMS, preferred_element_type=jnp.float32)
        dscores = (soft * (dprobs - delta) * SCALE).astype(jnp.bfloat16)
        part[m, g, :, :DH] = lax.dot_general(
            dscores, queries, TN_DIMS, preferred_element_type=jnp.float32
        ).astype(jnp.bfloat16)
        for step in range(1, ranks):

            @pl.when(me >= step)
            def _():
                part_copy(m, g, step - 1, lax.max(me - step, 0)).start()

        dq = jnp.dot(dscores, keys, preferred_element_type=jnp.float32)
        dq = jnp.concatenate([dq[h * tokens : (h + 1) * tokens] for h in range(GROUP)], axis=1)
        dquery[:, cols(g)] = dq
        weighed = stream[m, :, cols(g)].astype(jnp.float32) * gain[:, cols(g)]
        mean[...] += jnp.sum(weighed * dq, axis=-1, keepdims=True)

    def gather(m, g):
        rows = pl.ds(pl.multiple_of(me * tokens, tokens), tokens)
        total[...] = part[m, g, rows, :].astype(jnp.float32)
        for step in range(1, ranks):

            @pl.when(me < ranks - step)
            def _():
                part_copy(m, g, step - 1, lax.max(me - step, 0)).wait_recv()
                total[...] += landed[m, g, step - 1].astype(jnp.float32)

        rounded = total[...].astype(jnp.bfloat16)
        key_cols = pl.ds(pl.multiple_of(g * DH, DH), DH)
        value_cols = pl.ds(pl.multiple_of((KVH + g) * DH, DH), DH)
        dkv[m, :, key_cols] = rounded[:, :DH]
        dkv[m, :, value_cols] = rounded[:, DH:]
        wide = rounded.astype(jnp.float32)
        mean[...] += jnp.sum(
            wide[:, :DH] * keyval_raw[m, :, key_cols] + wide[:, DH:] * keyval_raw[m, :, value_cols],
            axis=-1,
            keepdims=True,
        )

    def project(m, g):
        back = lax.dot_general(
            dkv[m], weight[cols(g), :], NT_DIMS, preferred_element_type=jnp.float32
        )
        scaled = gain[:, cols(g)] * (dquery[:, cols(g)] + back)
        inv = inverse[m]
        pull = inv * inv * inv * (mean[...] * (1.0 / model))
        fresh = (
            up[m, :, cols(g)].astype(jnp.float32)
            + inv * scaled
            - stream[m, :, cols(g)].astype(jnp.float32) * pull
        )
        grads[m, :, cols(g)] = fresh.astype(jnp.bfloat16)

        @pl.when(sec > 0)
        def _():
            up_copy(m, g).start()

    def one_micro(m, carry):
        mean[...] = jnp.zeros_like(mean)
        pl.loop(0, KVH)(functools.partial(attend, m))
        pl.loop(0, KVH)(functools.partial(gather, m))
        for step in range(ranks - 1):
            dkv_copy(m, step).start()
        pl.loop(0, KVH)(functools.partial(project, m))
        return carry

    lax.fori_loop(0, micros, one_micro, 0)

    for m in range(micros):
        for step in range(ranks - 1):
            dkv_copy(m, step).wait_recv()

    rows = wgrad.shape[0]
    block = 256 if rows % 256 == 0 else rows

    @pl.loop(0, rows // block)
    def _(i):
        here = pl.ds(pl.multiple_of(i * block, block), block)
        acc = jnp.zeros((block, wgrad.shape[1]), jnp.float32)
        for m in range(micros):
            terms = jnp.concatenate([dkv[m]] + [dkv_all[m, s] for s in range(ranks - 1)], axis=0)
            acc += jnp.dot(normed_t[m, here, :], terms, preferred_element_type=jnp.float32)
        wgrad[here, :] = acc.astype(jnp.bfloat16)

    for m in range(micros):
        for step in range(ranks - 1):
            dkv_copy(m, step).wait_send()

    def drain(m, carry):
        def drain_group(g):
            @pl.when(sec > 0)
            def _():
                up_copy(m, g).wait_send()

            for step in range(1, ranks):

                @pl.when(me >= step)
                def _():
                    part_copy(m, g, step - 1, lax.max(me - step, 0)).wait_send()

        pl.loop(0, KVH)(drain_group)
        return carry

    lax.fori_loop(0, micros, drain, 0)


def shards(stream_in, gain, kv_weight, pattern, top_grad):
    sections = lax.axis_size("section")
    ranks = lax.axis_size("dp")
    rank = lax.axis_index("dp")
    stream = stream_in[0]
    micros, tokens, model = stream.shape
    weight = kv_weight[0]
    kv_width = weight.shape[1] // 2
    seq = tokens * ranks
    gain_f = gain.astype(jnp.float32)

    stream_f = stream.astype(jnp.float32)
    inverse = lax.rsqrt(jnp.mean(stream_f * stream_f, axis=-1, keepdims=True) + 1e-05)
    normed = (stream_f * inverse * gain_f[None]).astype(jnp.bfloat16)
    raw = jnp.dot(
        normed.reshape(micros * tokens, model), weight, preferred_element_type=jnp.float32
    ).reshape(micros, tokens, 2 * kv_width)
    keyval = lax.all_gather(raw.astype(jnp.bfloat16), "dp", axis=1, tiled=True)
    owned = lax.all_to_all(normed, "dp", split_axis=2, concat_axis=1, tiled=True)
    owned = owned.reshape(micros, ranks, tokens, model // ranks)
    order = lax.rem(rank - jnp.arange(ranks) + ranks, ranks)
    owned = jnp.take(owned, order, axis=1).reshape(micros, seq, model // ranks)
    normed_t = jnp.swapaxes(owned, 1, 2)

    tiles = seq // TILE
    query_pos = rank * tokens + jnp.arange(tokens)
    key_pos = jnp.arange(seq)
    seen = jnp.zeros((micros, tokens, seq), jnp.bool_)
    for row in range(tiles):
        for col in range(row + 1):
            pair = (query_pos[:, None] // TILE == row) & (key_pos[None, :] // TILE == col)
            seen = seen | (pair[None] & (pattern[:, row, col] > 0)[:, None, None])
    allowed = seen & (key_pos[None, :] <= query_pos[:, None])[None]

    queries = jnp.transpose(
        normed.reshape(micros, tokens, KVH, GROUP, DH), (0, 2, 3, 1, 4)
    ).reshape(micros, KVH, GROUP * tokens, DH)
    heads = keyval.reshape(micros, seq, 2, KVH, DH)
    scores = (
        jnp.einsum("mgqd,mkgd->mgqk", queries, heads[:, :, 0], preferred_element_type=jnp.float32)
        * SCALE
    ).reshape(micros, KVH, GROUP, tokens, seq)
    scores = jnp.where(allowed[:, None, None], scores, -1e30)
    expo = jnp.exp(scores - jnp.max(scores, axis=-1, keepdims=True))
    probs = (expo / jnp.sum(expo, axis=-1, keepdims=True)).reshape(
        micros, KVH, GROUP * tokens, seq
    )
    attn = jnp.einsum(
        "mgqk,mkgd->mgqd",
        probs.astype(jnp.bfloat16),
        heads[:, :, 1],
        preferred_element_type=jnp.float32,
    ).astype(jnp.bfloat16)

    vmem = pl.BlockSpec(memory_space=pltpu.VMEM)
    bf16, f32 = jnp.bfloat16, jnp.float32
    grads, wgrad = pl.pallas_call(
        functools.partial(relay, sections, ranks, micros, tokens),
        out_shape=(
            jax.ShapeDtypeStruct((micros, tokens, model), bf16),
            jax.ShapeDtypeStruct((model // ranks, 2 * kv_width), bf16),
        ),
        in_specs=[vmem] * 11,
        out_specs=(vmem, vmem),
        scratch_shapes=[
            pltpu.VMEM((micros, tokens, model), bf16),
            pltpu.VMEM((micros, KVH, seq, 2 * DH), bf16),
            pltpu.VMEM((micros, KVH, ranks - 1, tokens, 2 * DH), bf16),
            pltpu.VMEM((tokens, model), f32),
            pltpu.VMEM((tokens, 2 * DH), f32),
            pltpu.VMEM((micros, tokens, 2 * kv_width), bf16),
            pltpu.VMEM((micros, ranks - 1, tokens, 2 * kv_width), bf16),
            pltpu.VMEM((tokens, 1), f32),
            pltpu.SemaphoreType.DMA((micros, KVH)),
            pltpu.SemaphoreType.DMA((micros, KVH)),
            pltpu.SemaphoreType.DMA((micros, KVH, ranks - 1)),
            pltpu.SemaphoreType.DMA((micros, KVH, ranks - 1)),
            pltpu.SemaphoreType.DMA((micros, ranks - 1)),
            pltpu.SemaphoreType.DMA((micros, ranks - 1)),
        ],
        compiler_params=pltpu.CompilerParams(
            collective_id=0, has_side_effects=True, vmem_limit_bytes=60 * 1024 * 1024
        ),
    )(
        top_grad, stream, normed, inverse, gain_f, weight, keyval, probs, attn, raw / inverse,
        normed_t,
    )
    return grads[None], wgrad[None]


def solution(mesh):
    placed = (
        P("section", None, "dp", None),
        P("section", None),
        P("section", None, None),
        P(),
        P(None, "dp", None),
    )
    return jax.shard_map(
        shards,
        mesh=mesh,
        in_specs=placed,
        out_specs=(P("section", None, "dp", None), P("section", "dp", None)),
        check_vma=False,
    )
```

```python
import functools
import math

import jax
import jax.numpy as jnp
from jax import lax
from jax.experimental import pallas as pl
from jax.experimental.pallas import tpu as pltpu
from jax.sharding import PartitionSpec as P

H = 48
DH = 128
KVH = 4
TILE = 128
GROUP = H // KVH
SCALE = 1.0 / math.sqrt(DH)
MESH = pl.DeviceIdType.MESH
NT_DIMS = (((1,), (1,)), ((), ()))
TN_DIMS = (((0,), (0,)), ((), ()))


def relay(
    sections, ranks, micros, tokens,
    top, stream, gain, weight_hbm, mask,
    grads, wgrad,
    weight, normed, inverse, keyval_own, keyval, keyval_raw, probs, attn, owned,
    up, part, landed, dquery, total, dkv_all, mean,
    weight_sem, keyval_send, keyval_recv, owned_send, owned_recv,
    up_send, up_recv, part_send, part_recv, dkv_send, dkv_recv,
):
    sec = lax.axis_index("section")
    me = lax.axis_index("dp")
    width = GROUP * DH
    model = width * KVH
    seq = ranks * tokens
    share = model // ranks
    f32, bf16 = jnp.float32, jnp.bfloat16

    def cols(g):
        return pl.ds(pl.multiple_of(g * width, 128), width)

    def key_cols(g):
        return pl.ds(pl.multiple_of(g * DH, DH), DH)

    def value_cols(g):
        return pl.ds(pl.multiple_of((KVH + g) * DH, DH), DH)

    def rank_rows(rank):
        return pl.ds(pl.multiple_of(rank * tokens, tokens), tokens)

    def share_cols(rank):
        return pl.ds(pl.multiple_of(rank * share, 128), share)

    def weight_copy(g):
        return pltpu.make_async_copy(
            weight_hbm.at[cols(g), :], weight.at[cols(g), :], weight_sem.at[g]
        )

    def keyval_copy(step):
        return pltpu.make_async_remote_copy(
            src_ref=keyval_own,
            dst_ref=keyval.at[:, rank_rows(me), :],
            send_sem=keyval_send.at[step - 1],
            recv_sem=keyval_recv.at[step - 1],
            device_id=(sec, lax.rem(me + step, ranks)),
            device_id_type=MESH,
        )

    def owned_copy(step):
        peer = lax.rem(me + step, ranks)
        return pltpu.make_async_remote_copy(
            src_ref=normed.at[:, :, share_cols(peer)],
            dst_ref=owned.at[:, step],
            send_sem=owned_send.at[step - 1],
            recv_sem=owned_recv.at[step - 1],
            device_id=(sec, peer),
            device_id_type=MESH,
        )

    def stacked(block):
        return jnp.concatenate([block[:, h * DH : (h + 1) * DH] for h in range(GROUP)], axis=0)

    barrier = pltpu.get_barrier_semaphore()
    for step in (1, sections - 1):
        pl.semaphore_signal(
            barrier, inc=1, device_id=(lax.rem(sec + step, sections), me), device_id_type=MESH
        )
    for step in range(1, ranks):
        pl.semaphore_signal(
            barrier, inc=1, device_id=(sec, lax.rem(me + step, ranks)), device_id_type=MESH
        )
    for g in range(KVH):
        weight_copy(g).start()

    def normalize(m, carry):
        mean[...] = jnp.zeros_like(mean)

        @pl.loop(0, KVH)
        def _(g):
            wide = stream[m, :, cols(g)].astype(f32)
            mean[...] += jnp.sum(wide * wide, axis=-1, keepdims=True)

        inverse[m] = lax.rsqrt(mean[...] * (1.0 / model) + 1e-05)

        @pl.loop(0, KVH)
        def _(g):
            wide = stream[m, :, cols(g)].astype(f32)
            normed[m, :, cols(g)] = (wide * inverse[m] * gain[:, cols(g)]).astype(bf16)

        return carry

    lax.fori_loop(0, micros, normalize, 0)
    keyval_raw[...] = jnp.zeros_like(keyval_raw)

    @pl.loop(0, KVH)
    def _(g):
        weight_copy(g).wait()
        rows = normed[:, :, cols(g)].reshape(micros * tokens, width)
        keyval_raw[...] += jnp.dot(
            rows, weight[cols(g), :], preferred_element_type=f32
        ).reshape(keyval_raw.shape)

    keyval_own[...] = keyval_raw[...].astype(bf16)
    pl.semaphore_wait(barrier, 2 + ranks - 1)
    for step in range(1, ranks):

        @pl.when(me < ranks - step)
        def _():
            keyval_copy(step).start()

    for m in range(micros):
        keyval_raw[m] = keyval_raw[m] / inverse[m]
        keyval[m, rank_rows(me), :] = keyval_own[m]
        owned[m, 0] = normed[m, :, share_cols(me)]
    for rank in range(1, ranks):

        @pl.when(me < rank)
        def _():
            keyval[:, rank * tokens : (rank + 1) * tokens, :] = jnp.zeros(
                (micros, tokens, keyval.shape[2]), bf16
            )

    for step in range(1, ranks):

        @pl.when(me >= step)
        def _():
            keyval_copy(step).wait_recv()

    @pl.when(sec < sections - 1)
    def _():
        for step in range(1, ranks):
            owned_copy(step).start()

    def forward(m, carry):
        @pl.loop(0, KVH)
        def _(g):
            queries = stacked(normed[m, :, cols(g)])
            scores = (
                lax.dot_general(
                    keyval[m, :, key_cols(g)], queries, NT_DIMS, preferred_element_type=f32
                )
                * SCALE
            )
            seen = jnp.concatenate([mask[m]] * (GROUP * tokens // mask.shape[2]), axis=1)
            scores = jnp.where(seen > 0.5, scores, -1e30)
            expo = jnp.exp(scores - jnp.max(scores, axis=0, keepdims=True))
            soft = expo / jnp.sum(expo, axis=0, keepdims=True)
            probs[m, g] = soft
            attn[m, g] = lax.dot_general(
                soft.astype(bf16), keyval[m, :, value_cols(g)], TN_DIMS, preferred_element_type=f32
            ).astype(bf16)

        return carry

    lax.fori_loop(0, micros, forward, 0)

    @pl.when(sec == sections - 1)
    def _():
        up[...] = top[...]

    def up_copy(m, g):
        return pltpu.make_async_remote_copy(
            src_ref=grads.at[m, :, cols(g)],
            dst_ref=up.at[m, :, cols(g)],
            send_sem=up_send.at[m, g],
            recv_sem=up_recv.at[m, g],
            device_id=(lax.rem(sec + sections - 1, sections), me),
            device_id_type=MESH,
        )

    def part_copy(m, g, slot, peer):
        return pltpu.make_async_remote_copy(
            src_ref=part.at[m, g, rank_rows(peer), :],
            dst_ref=landed.at[m, g, slot],
            send_sem=part_send.at[m, g, slot],
            recv_sem=part_recv.at[m, g, slot],
            device_id=(sec, peer),
            device_id_type=MESH,
        )

    def dkv_copy(m, step):
        return pltpu.make_async_remote_copy(
            src_ref=dkv_all.at[m, 0],
            dst_ref=dkv_all.at[m, step + 1],
            send_sem=dkv_send.at[m, step],
            recv_sem=dkv_recv.at[m, step],
            device_id=(sec, lax.rem(me + step + 1, ranks)),
            device_id_type=MESH,
        )

    def attend(m, g):
        @pl.when(sec < sections - 1)
        def _():
            up_copy(m, g).wait_recv()

        ups = stacked(up[m, :, cols(g)])
        queries = stacked(normed[m, :, cols(g)])
        keys = keyval[m, :, key_cols(g)]
        values = keyval[m, :, value_cols(g)]
        product = ups.astype(f32) * attn[m, g].astype(f32)
        high = product.astype(bf16)
        low = (product - high.astype(f32)).astype(bf16)
        delta = lax.dot_general(
            jnp.ones((16, 2 * DH), bf16),
            jnp.concatenate([high, low], axis=1),
            NT_DIMS,
            preferred_element_type=f32,
        )[:1]
        soft = probs[m, g]
        dprobs = lax.dot_general(values, ups, NT_DIMS, preferred_element_type=f32)
        dscores = (soft * (dprobs - delta) * SCALE).astype(bf16)
        part[m, g, :, DH:] = jnp.dot(
            soft.astype(bf16), ups, preferred_element_type=f32
        ).astype(bf16)
        part[m, g, :, :DH] = jnp.dot(dscores, queries, preferred_element_type=f32).astype(bf16)
        for step in range(1, ranks):

            @pl.when(me >= step)
            def _():
                part_copy(m, g, step - 1, lax.max(me - step, 0)).start()

        dq = lax.dot_general(dscores, keys, TN_DIMS, preferred_element_type=f32)
        dq = jnp.concatenate([dq[h * tokens : (h + 1) * tokens] for h in range(GROUP)], axis=1)
        dquery[:, cols(g)] = dq
        weighed = stream[m, :, cols(g)].astype(jnp.float32) * gain[:, cols(g)]
        mean[...] += jnp.sum(weighed * dq, axis=-1, keepdims=True)

    def gather(m, g):
        total[...] = part[m, g, rank_rows(me), :].astype(jnp.float32)
        for step in range(1, ranks):

            @pl.when(me < ranks - step)
            def _():
                part_copy(m, g, step - 1, lax.max(me - step, 0)).wait_recv()
                total[...] += landed[m, g, step - 1].astype(jnp.float32)

        rounded = total[...].astype(jnp.bfloat16)
        dkv_all[m, 0, :, key_cols(g)] = rounded[:, :DH]
        dkv_all[m, 0, :, value_cols(g)] = rounded[:, DH:]
        wide = rounded.astype(jnp.float32)
        mean[...] += jnp.sum(
            wide[:, :DH] * keyval_raw[m, :, key_cols(g)]
            + wide[:, DH:] * keyval_raw[m, :, value_cols(g)],
            axis=-1,
            keepdims=True,
        )

    def project(m, g):
        back = lax.dot_general(
            dkv_all[m, 0], weight[cols(g), :], NT_DIMS, preferred_element_type=jnp.float32
        )
        scaled = gain[:, cols(g)] * (dquery[:, cols(g)] + back)
        inv = inverse[m]
        pull = inv * inv * inv * (mean[...] * (1.0 / model))
        fresh = (
            up[m, :, cols(g)].astype(jnp.float32)
            + inv * scaled
            - stream[m, :, cols(g)].astype(jnp.float32) * pull
        )
        grads[m, :, cols(g)] = fresh.astype(jnp.bfloat16)

        @pl.when(sec > 0)
        def _():
            up_copy(m, g).start()

    def one_micro(m, carry):
        mean[...] = jnp.zeros_like(mean)
        pl.loop(0, KVH)(functools.partial(attend, m))
        pl.loop(0, KVH)(functools.partial(gather, m))
        for step in range(ranks - 1):
            dkv_copy(m, step).start()
        pl.loop(0, KVH)(functools.partial(project, m))
        return carry

    lax.fori_loop(0, micros, one_micro, 0)

    @pl.when(sec == sections - 1)
    def _():
        for step in range(1, ranks):
            owned_copy(step).start()

    for step in range(1, ranks):
        owned_copy(step).wait_recv()
    for m in range(micros):
        for step in range(ranks - 1):
            dkv_copy(m, step).wait_recv()

    block = 256 if share % 256 == 0 else share

    @pl.loop(0, share // block)
    def _(i):
        here = pl.ds(pl.multiple_of(i * block, block), block)
        wgrad[here, :] = lax.dot_general(
            owned[:, :, :, here].reshape(micros * seq, block),
            dkv_all[...].reshape(micros * seq, wgrad.shape[1]),
            TN_DIMS,
            preferred_element_type=f32,
        ).astype(bf16)

    for step in range(1, ranks):
        owned_copy(step).wait_send()

        @pl.when(me < ranks - step)
        def _():
            keyval_copy(step).wait_send()

    for m in range(micros):
        for step in range(ranks - 1):
            dkv_copy(m, step).wait_send()

    def drain(m, carry):
        def drain_group(g):
            @pl.when(sec > 0)
            def _():
                up_copy(m, g).wait_send()

            for step in range(1, ranks):

                @pl.when(me >= step)
                def _():
                    part_copy(m, g, step - 1, lax.max(me - step, 0)).wait_send()

        pl.loop(0, KVH)(drain_group)
        return carry

    lax.fori_loop(0, micros, drain, 0)


def shards(stream_in, gain, kv_weight, pattern, top_grad):
    sections = lax.axis_size("section")
    ranks = lax.axis_size("dp")
    rank = lax.axis_index("dp")
    stream = stream_in[0]
    micros, tokens, model = stream.shape
    weight = kv_weight[0]
    kv_width = weight.shape[1] // 2
    seq = tokens * ranks

    tiles = seq // TILE
    query_pos = rank * tokens + jnp.arange(tokens)
    key_pos = jnp.arange(seq)
    seen = jnp.zeros((micros, tokens, seq), jnp.bool_)
    for row in range(tiles):
        for col in range(row + 1):
            pair = (query_pos[:, None] // TILE == row) & (key_pos[None, :] // TILE == col)
            seen = seen | (pair[None] & (pattern[:, row, col] > 0)[:, None, None])
    allowed = seen & (key_pos[None, :] <= query_pos[:, None])[None]

    mask = jnp.swapaxes(allowed, 1, 2).astype(jnp.float32)
    mask = jnp.tile(mask, (1, 1, max(1, DH // tokens)))

    vmem = pl.BlockSpec(memory_space=pltpu.VMEM)
    bf16, f32 = jnp.bfloat16, jnp.float32
    grads, wgrad = pl.pallas_call(
        functools.partial(relay, sections, ranks, micros, tokens),
        out_shape=(
            jax.ShapeDtypeStruct((micros, tokens, model), bf16),
            jax.ShapeDtypeStruct((model // ranks, 2 * kv_width), bf16),
        ),
        in_specs=[vmem, vmem, vmem, pl.BlockSpec(memory_space=pl.ANY), vmem],
        out_specs=(vmem, vmem),
        scratch_shapes=[
            pltpu.VMEM((model, 2 * kv_width), bf16),
            pltpu.VMEM((micros, tokens, model), bf16),
            pltpu.VMEM((micros, tokens, 1), f32),
            pltpu.VMEM((micros, tokens, 2 * kv_width), bf16),
            pltpu.VMEM((micros, seq, 2 * kv_width), bf16),
            pltpu.VMEM((micros, tokens, 2 * kv_width), f32),
            pltpu.VMEM((micros, KVH, seq, GROUP * tokens), f32),
            pltpu.VMEM((micros, KVH, GROUP * tokens, DH), bf16),
            pltpu.VMEM((micros, ranks, tokens, model // ranks), bf16),
            pltpu.VMEM((micros, tokens, model), bf16),
            pltpu.VMEM((micros, KVH, seq, 2 * DH), bf16),
            pltpu.VMEM((micros, KVH, ranks - 1, tokens, 2 * DH), bf16),
            pltpu.VMEM((tokens, model), f32),
            pltpu.VMEM((tokens, 2 * DH), f32),
            pltpu.VMEM((micros, ranks, tokens, 2 * kv_width), bf16),
            pltpu.VMEM((tokens, 1), f32),
            pltpu.SemaphoreType.DMA((KVH,)),
            pltpu.SemaphoreType.DMA((ranks - 1,)),
            pltpu.SemaphoreType.DMA((ranks - 1,)),
            pltpu.SemaphoreType.DMA((ranks - 1,)),
            pltpu.SemaphoreType.DMA((ranks - 1,)),
            pltpu.SemaphoreType.DMA((micros, KVH)),
            pltpu.SemaphoreType.DMA((micros, KVH)),
            pltpu.SemaphoreType.DMA((micros, KVH, ranks - 1)),
            pltpu.SemaphoreType.DMA((micros, KVH, ranks - 1)),
            pltpu.SemaphoreType.DMA((micros, ranks - 1)),
            pltpu.SemaphoreType.DMA((micros, ranks - 1)),
        ],
        compiler_params=pltpu.CompilerParams(
            collective_id=0, has_side_effects=True, vmem_limit_bytes=60 * 1024 * 1024
        ),
    )(top_grad, stream, gain.astype(f32), weight, mask)
    return grads[None], wgrad[None]


def solution(mesh):
    placed = (
        P("section", None, "dp", None),
        P("section", None),
        P("section", None, None),
        P(),
        P(None, "dp", None),
    )
    return jax.shard_map(
        shards,
        mesh=mesh,
        in_specs=placed,
        out_specs=(P("section", None, "dp", None), P("section", "dp", None)),
        check_vma=False,
    )
```

```python
import functools
import math

import jax
import jax.numpy as jnp
from jax import lax
from jax.experimental import pallas as pl
from jax.experimental.pallas import tpu as pltpu
from jax.sharding import PartitionSpec as P

H = 48
DH = 128
KVH = 4
TILE = 128
GROUP = H // KVH
SCALE = 1.0 / math.sqrt(DH)
MESH = pl.DeviceIdType.MESH
NT_DIMS = (((1,), (1,)), ((), ()))
TN_DIMS = (((0,), (0,)), ((), ()))


def relay(
    sections, ranks, micros, tokens,
    top, stream, gain, weight_hbm, mask,
    grads, wgrad,
    weight, normed, inverse, keyval_own, keyval, keyval_raw, probs, attn, owned,
    up, part, landed, base, dkv_all, mean,
    weight_sem, keyval_send, keyval_recv, owned_send, owned_recv,
    up_send, up_recv, part_send, part_recv, dkv_send, dkv_recv,
):
    sec = lax.axis_index("section")
    me = lax.axis_index("dp")
    width = GROUP * DH
    model = width * KVH
    seq = ranks * tokens
    share = model // ranks
    f32, bf16 = jnp.float32, jnp.bfloat16

    def span(low, size):
        return pl.ds(low if isinstance(low, int) else pl.multiple_of(low, 128), size)

    def cols(g):
        return span(g * width, width)

    def key_cols(g):
        return span(g * DH, DH)

    def value_cols(g):
        return span((KVH + g) * DH, DH)

    def rank_rows(rank):
        return pl.ds(pl.multiple_of(rank * tokens, tokens), tokens)

    def share_cols(rank):
        return pl.ds(pl.multiple_of(rank * share, 128), share)

    def weight_copy(g):
        return pltpu.make_async_copy(
            weight_hbm.at[cols(g), :], weight.at[cols(g), :], weight_sem.at[g]
        )

    def keyval_copy(m, step):
        return pltpu.make_async_remote_copy(
            src_ref=keyval_own.at[m],
            dst_ref=keyval.at[m, rank_rows(me), :],
            send_sem=keyval_send.at[m, step - 1],
            recv_sem=keyval_recv.at[m, step - 1],
            device_id=(sec, lax.rem(me + step, ranks)),
            device_id_type=MESH,
        )

    def owned_copy(step):
        peer = lax.rem(me + step, ranks)
        return pltpu.make_async_remote_copy(
            src_ref=normed.at[:, :, share_cols(peer)],
            dst_ref=owned.at[:, step],
            send_sem=owned_send.at[step - 1],
            recv_sem=owned_recv.at[step - 1],
            device_id=(sec, peer),
            device_id_type=MESH,
        )

    def stacked(block):
        return jnp.concatenate([block[:, h * DH : (h + 1) * DH] for h in range(GROUP)], axis=0)

    barrier = pltpu.get_barrier_semaphore()
    for step in (1, sections - 1):
        pl.semaphore_signal(
            barrier, inc=1, device_id=(lax.rem(sec + step, sections), me), device_id_type=MESH
        )
    for step in range(1, ranks):
        pl.semaphore_signal(
            barrier, inc=1, device_id=(sec, lax.rem(me + step, ranks)), device_id_type=MESH
        )
    for g in range(KVH):
        weight_copy(g).start()

    def normalize(m, carry):
        mean[...] = jnp.zeros_like(mean)

        @pl.loop(0, KVH)
        def _(g):
            wide = stream[m, :, cols(g)].astype(f32)
            mean[...] += jnp.sum(wide * wide, axis=-1, keepdims=True)

        inverse[m] = lax.rsqrt(mean[...] * (1.0 / model) + 1e-05)

        @pl.loop(0, KVH)
        def _(g):
            wide = stream[m, :, cols(g)].astype(f32)
            normed[m, :, cols(g)] = (wide * inverse[m] * gain[:, cols(g)]).astype(bf16)

        return carry

    lax.fori_loop(0, micros, normalize, 0)
    keyval_raw[...] = jnp.zeros_like(keyval_raw)

    @pl.loop(0, KVH)
    def _(g):
        weight_copy(g).wait()
        rows = normed[:, :, cols(g)].reshape(micros * tokens, width)
        keyval_raw[...] += jnp.dot(
            rows, weight[cols(g), :], preferred_element_type=f32
        ).reshape(keyval_raw.shape)

    keyval_own[...] = keyval_raw[...].astype(bf16)
    pl.semaphore_wait(barrier, 2 + ranks - 1)
    for m in range(micros):
        for step in range(1, ranks):

            @pl.when(me < ranks - step)
            def _():
                keyval_copy(m, step).start()

    for m in range(micros):
        keyval_raw[m] = keyval_raw[m] / inverse[m]
        keyval[m, rank_rows(me), :] = keyval_own[m]
        owned[m, 0] = normed[m, :, share_cols(me)]
    for rank in range(1, ranks):

        @pl.when(me < rank)
        def _():
            keyval[:, rank * tokens : (rank + 1) * tokens, :] = jnp.zeros(
                (micros, tokens, keyval.shape[2]), bf16
            )

    for step in range(1, ranks):

        @pl.when(me >= ranks - step)
        def _():
            landed[:, :, step - 1] = jnp.zeros((micros, KVH, tokens, 2 * DH), bf16)

    @pl.when(sec < sections - 2)
    def _():
        for step in range(1, ranks):
            owned_copy(step).start()

    def forward(m, carry):
        for step in range(1, ranks):

            @pl.when(me >= step)
            def _():
                keyval_copy(m, step).wait_recv()

        @pl.loop(0, KVH)
        def _(g):
            queries = stacked(normed[m, :, cols(g)])
            scores = (
                lax.dot_general(
                    keyval[m, :, key_cols(g)], queries, NT_DIMS, preferred_element_type=f32
                )
                * SCALE
            )
            seen = jnp.concatenate([mask[m]] * (GROUP * tokens // mask.shape[2]), axis=1)
            scores = jnp.where(seen > 0.5, scores, -1e30)
            expo = jnp.exp(scores - jnp.max(scores, axis=0, keepdims=True))
            soft = expo / jnp.sum(expo, axis=0, keepdims=True)
            probs[m, g] = soft
            attn[m, g] = lax.dot_general(
                soft.astype(bf16), keyval[m, :, value_cols(g)], TN_DIMS, preferred_element_type=f32
            ).astype(bf16)

        return carry

    @pl.when(sec < sections - 1)
    def _():
        lax.fori_loop(0, micros, forward, 0)

    @pl.when(sec == sections - 1)
    def _():
        up[...] = top[...]

    def up_copy(m, g):
        return pltpu.make_async_remote_copy(
            src_ref=grads.at[m, :, cols(g)],
            dst_ref=up.at[m, :, cols(g)],
            send_sem=up_send.at[m, g],
            recv_sem=up_recv.at[m, g],
            device_id=(lax.rem(sec + sections - 1, sections), me),
            device_id_type=MESH,
        )

    def part_copy(m, g, slot, peer):
        return pltpu.make_async_remote_copy(
            src_ref=part.at[m, g, rank_rows(peer), :],
            dst_ref=landed.at[m, g, slot],
            send_sem=part_send.at[m, g, slot],
            recv_sem=part_recv.at[m, g, slot],
            device_id=(sec, peer),
            device_id_type=MESH,
        )

    def dkv_copy(m, step):
        return pltpu.make_async_remote_copy(
            src_ref=dkv_all.at[m, 0],
            dst_ref=dkv_all.at[m, step + 1],
            send_sem=dkv_send.at[m, step],
            recv_sem=dkv_recv.at[m, step],
            device_id=(sec, lax.rem(me + step + 1, ranks)),
            device_id_type=MESH,
        )

    def attend(m, g):
        @pl.when(sec < sections - 1)
        def _():
            up_copy(m, g).wait_recv()

        ups = stacked(up[m, :, cols(g)])
        queries = stacked(normed[m, :, cols(g)])
        keys = keyval[m, :, key_cols(g)]
        values = keyval[m, :, value_cols(g)]
        product = ups.astype(f32) * attn[m, g].astype(f32)
        high = product.astype(bf16)
        low = (product - high.astype(f32)).astype(bf16)
        delta = lax.dot_general(
            jnp.ones((16, 2 * DH), bf16),
            jnp.concatenate([high, low], axis=1),
            NT_DIMS,
            preferred_element_type=f32,
        )[:1]
        soft = probs[m, g]
        dprobs = lax.dot_general(values, ups, NT_DIMS, preferred_element_type=f32)
        dscores = (soft * (dprobs - delta) * SCALE).astype(bf16)
        part[m, g, :, DH:] = jnp.dot(
            soft.astype(bf16), ups, preferred_element_type=f32
        ).astype(bf16)
        part[m, g, :, :DH] = jnp.dot(dscores, queries, preferred_element_type=f32).astype(bf16)
        for step in range(1, ranks):

            @pl.when(me >= step)
            def _():
                part_copy(m, g, step - 1, lax.max(me - step, 0)).start()

        dq = lax.dot_general(dscores, keys, TN_DIMS, preferred_element_type=f32)
        dq = jnp.concatenate([dq[h * tokens : (h + 1) * tokens] for h in range(GROUP)], axis=1)
        scaled = gain[:, cols(g)] * dq
        mean[...] += jnp.sum(
            stream[m, :, cols(g)].astype(f32) * scaled, axis=-1, keepdims=True
        )
        base[:, cols(g)] = up[m, :, cols(g)].astype(f32) + inverse[m] * scaled

    def gather(m, g):
        for step in range(1, ranks):

            @pl.when(me < ranks - step)
            def _():
                part_copy(m, g, step - 1, lax.max(me - step, 0)).wait_recv()

        terms = part[m, g, rank_rows(me), :].astype(f32)
        for step in range(1, ranks):
            terms = terms + landed[m, g, step - 1].astype(f32)
        rounded = terms.astype(bf16)
        dkv_all[m, 0, :, key_cols(g)] = rounded[:, :DH]
        dkv_all[m, 0, :, value_cols(g)] = rounded[:, DH:]
        wide = rounded.astype(jnp.float32)
        return (
            wide[:, :DH] * keyval_raw[m, :, key_cols(g)]
            + wide[:, DH:] * keyval_raw[m, :, value_cols(g)]
        )

    def project(m, g, inv, pull):
        back = lax.dot_general(
            dkv_all[m, 0], weight[cols(g), :], NT_DIMS, preferred_element_type=jnp.float32
        )
        fresh = (
            base[:, cols(g)]
            + inv * (gain[:, cols(g)] * back)
            - stream[m, :, cols(g)].astype(f32) * pull
        )
        grads[m, :, cols(g)] = fresh.astype(jnp.bfloat16)

        @pl.when(sec > 0)
        def _():
            up_copy(m, g).start()

    def one_micro(m, carry):
        @pl.when(sec == sections - 1)
        def _():
            forward(m, carry)

        mean[...] = jnp.zeros_like(mean)
        pl.loop(0, KVH)(functools.partial(attend, m))
        pulls = gather(m, 0)
        for g in range(1, KVH):
            pulls = pulls + gather(m, g)
        for step in range(ranks - 1):
            dkv_copy(m, step).start()
        inv = inverse[m]
        mean_all = mean[...] + jnp.sum(pulls, axis=-1, keepdims=True)
        pull = inv * inv * inv * (mean_all * (1.0 / model))
        for g in range(KVH):
            project(m, g, inv, pull)
        return carry

    lax.fori_loop(0, micros, one_micro, 0)

    @pl.when(sec >= sections - 2)
    def _():
        for step in range(1, ranks):
            owned_copy(step).start()

    for step in range(1, ranks):
        owned_copy(step).wait_recv()
    for m in range(micros):
        for step in range(ranks - 1):
            dkv_copy(m, step).wait_recv()

    block = 256 if share % 256 == 0 else share

    @pl.loop(0, share // block)
    def _(i):
        here = pl.ds(pl.multiple_of(i * block, block), block)
        wgrad[here, :] = lax.dot_general(
            owned[:, :, :, here].reshape(micros * seq, block),
            dkv_all[...].reshape(micros * seq, wgrad.shape[1]),
            TN_DIMS,
            preferred_element_type=f32,
        ).astype(bf16)

    for step in range(1, ranks):
        owned_copy(step).wait_send()

        @pl.when(me < ranks - step)
        def _():
            for m in range(micros):
                keyval_copy(m, step).wait_send()

    for m in range(micros):
        for step in range(ranks - 1):
            dkv_copy(m, step).wait_send()

    def drain(m, carry):
        def drain_group(g):
            @pl.when(sec > 0)
            def _():
                up_copy(m, g).wait_send()

            for step in range(1, ranks):

                @pl.when(me >= step)
                def _():
                    part_copy(m, g, step - 1, lax.max(me - step, 0)).wait_send()

        pl.loop(0, KVH)(drain_group)
        return carry

    lax.fori_loop(0, micros, drain, 0)


def shards(stream_in, gain, kv_weight, pattern, top_grad):
    sections = lax.axis_size("section")
    ranks = lax.axis_size("dp")
    rank = lax.axis_index("dp")
    stream = stream_in[0]
    micros, tokens, model = stream.shape
    weight = kv_weight[0]
    kv_width = weight.shape[1] // 2
    seq = tokens * ranks

    tiles = seq // TILE
    query_pos = rank * tokens + jnp.arange(tokens)
    key_pos = jnp.arange(seq)
    seen = jnp.zeros((micros, tokens, seq), jnp.bool_)
    for row in range(tiles):
        for col in range(row + 1):
            pair = (query_pos[:, None] // TILE == row) & (key_pos[None, :] // TILE == col)
            seen = seen | (pair[None] & (pattern[:, row, col] > 0)[:, None, None])
    allowed = seen & (key_pos[None, :] <= query_pos[:, None])[None]

    mask = jnp.swapaxes(allowed, 1, 2).astype(jnp.float32)
    mask = jnp.tile(mask, (1, 1, max(1, DH // tokens)))

    vmem = pl.BlockSpec(memory_space=pltpu.VMEM)
    bf16, f32 = jnp.bfloat16, jnp.float32
    grads, wgrad = pl.pallas_call(
        functools.partial(relay, sections, ranks, micros, tokens),
        out_shape=(
            jax.ShapeDtypeStruct((micros, tokens, model), bf16),
            jax.ShapeDtypeStruct((model // ranks, 2 * kv_width), bf16),
        ),
        in_specs=[vmem, vmem, vmem, pl.BlockSpec(memory_space=pl.ANY), vmem],
        out_specs=(vmem, vmem),
        scratch_shapes=[
            pltpu.VMEM((model, 2 * kv_width), bf16),
            pltpu.VMEM((micros, tokens, model), bf16),
            pltpu.VMEM((micros, tokens, 1), f32),
            pltpu.VMEM((micros, tokens, 2 * kv_width), bf16),
            pltpu.VMEM((micros, seq, 2 * kv_width), bf16),
            pltpu.VMEM((micros, tokens, 2 * kv_width), f32),
            pltpu.VMEM((micros, KVH, seq, GROUP * tokens), f32),
            pltpu.VMEM((micros, KVH, GROUP * tokens, DH), bf16),
            pltpu.VMEM((micros, ranks, tokens, model // ranks), bf16),
            pltpu.VMEM((micros, tokens, model), bf16),
            pltpu.VMEM((micros, KVH, seq, 2 * DH), bf16),
            pltpu.VMEM((micros, KVH, ranks - 1, tokens, 2 * DH), bf16),
            pltpu.VMEM((tokens, model), f32),
            pltpu.VMEM((micros, ranks, tokens, 2 * kv_width), bf16),
            pltpu.VMEM((tokens, 1), f32),
            pltpu.SemaphoreType.DMA((KVH,)),
            pltpu.SemaphoreType.DMA((micros, ranks - 1)),
            pltpu.SemaphoreType.DMA((micros, ranks - 1)),
            pltpu.SemaphoreType.DMA((ranks - 1,)),
            pltpu.SemaphoreType.DMA((ranks - 1,)),
            pltpu.SemaphoreType.DMA((micros, KVH)),
            pltpu.SemaphoreType.DMA((micros, KVH)),
            pltpu.SemaphoreType.DMA((micros, KVH, ranks - 1)),
            pltpu.SemaphoreType.DMA((micros, KVH, ranks - 1)),
            pltpu.SemaphoreType.DMA((micros, ranks - 1)),
            pltpu.SemaphoreType.DMA((micros, ranks - 1)),
        ],
        compiler_params=pltpu.CompilerParams(
            collective_id=0, has_side_effects=True, vmem_limit_bytes=60 * 1024 * 1024
        ),
    )(top_grad, stream, gain.astype(f32), weight, mask)
    return grads[None], wgrad[None]


def solution(mesh):
    placed = (
        P("section", None, "dp", None),
        P("section", None),
        P("section", None, None),
        P(),
        P(None, "dp", None),
    )
    return jax.shard_map(
        shards,
        mesh=mesh,
        in_specs=placed,
        out_specs=(P("section", None, "dp", None), P("section", "dp", None)),
        check_vma=False,
    )
```

```python
import functools
import math

import jax
import jax.numpy as jnp
from jax import lax
from jax.experimental import pallas as pl
from jax.experimental.pallas import tpu as pltpu
from jax.sharding import PartitionSpec as P

H = 48
DH = 128
KVH = 4
TILE = 128
GROUP = H // KVH
SCALE = 1.0 / math.sqrt(DH)
MESH = pl.DeviceIdType.MESH
NT_DIMS = (((1,), (1,)), ((), ()))
TN_DIMS = (((0,), (0,)), ((), ()))


def relay(
    sections, ranks, micros, tokens,
    top, stream, gain, weight_hbm, mask,
    grads, wgrad,
    weight, normed, inverse, keyval_own, keyval, keyval_raw, probs, attn, owned,
    up, part, landed, base, dkv_all, mean,
    weight_sem, keyval_send, keyval_recv, owned_send, owned_recv,
    up_send, up_recv, part_send, part_recv, dkv_send, dkv_recv,
):
    sec = lax.axis_index("section")
    me = lax.axis_index("dp")
    width = GROUP * DH
    model = width * KVH
    seq = ranks * tokens
    share = model // ranks
    f32, bf16 = jnp.float32, jnp.bfloat16

    def span(low, size):
        return pl.ds(low if isinstance(low, int) else pl.multiple_of(low, 128), size)

    def cols(g):
        return span(g * width, width)

    def key_cols(g):
        return span(g * DH, DH)

    def value_cols(g):
        return span((KVH + g) * DH, DH)

    def rank_rows(rank):
        return pl.ds(pl.multiple_of(rank * tokens, tokens), tokens)

    def share_cols(rank):
        return pl.ds(pl.multiple_of(rank * share, 128), share)

    def weight_copy(g):
        return pltpu.make_async_copy(
            weight_hbm.at[cols(g), :], weight.at[cols(g), :], weight_sem.at[g]
        )

    def keyval_copy(m, step):
        return pltpu.make_async_remote_copy(
            src_ref=keyval_own.at[m],
            dst_ref=keyval.at[m, rank_rows(me), :],
            send_sem=keyval_send.at[m, step - 1],
            recv_sem=keyval_recv.at[m, step - 1],
            device_id=(sec, lax.rem(me + step, ranks)),
            device_id_type=MESH,
        )

    def owned_copy(step):
        peer = lax.rem(me + step, ranks)
        return pltpu.make_async_remote_copy(
            src_ref=normed.at[:, :, share_cols(peer)],
            dst_ref=owned.at[:, step],
            send_sem=owned_send.at[step - 1],
            recv_sem=owned_recv.at[step - 1],
            device_id=(sec, peer),
            device_id_type=MESH,
        )

    def stacked(block):
        return jnp.concatenate([block[:, h * DH : (h + 1) * DH] for h in range(GROUP)], axis=0)

    barrier = pltpu.get_barrier_semaphore()
    for step in (1, sections - 1):
        pl.semaphore_signal(
            barrier, inc=1, device_id=(lax.rem(sec + step, sections), me), device_id_type=MESH
        )
    for step in range(1, ranks):
        pl.semaphore_signal(
            barrier, inc=1, device_id=(sec, lax.rem(me + step, ranks)), device_id_type=MESH
        )
    for g in range(KVH):
        weight_copy(g).start()

    def normalize(m, carry):
        mean[...] = jnp.zeros_like(mean)

        @pl.loop(0, KVH)
        def _(g):
            wide = stream[m, :, cols(g)].astype(f32)
            mean[...] += jnp.sum(wide * wide, axis=-1, keepdims=True)

        inverse[m] = lax.rsqrt(mean[...] * (1.0 / model) + 1e-05)

        @pl.loop(0, KVH)
        def _(g):
            wide = stream[m, :, cols(g)].astype(f32)
            normed[m, :, cols(g)] = (wide * inverse[m] * gain[:, cols(g)]).astype(bf16)

        return carry

    lax.fori_loop(0, micros, normalize, 0)
    keyval_raw[...] = jnp.zeros_like(keyval_raw)

    @pl.loop(0, KVH)
    def _(g):
        weight_copy(g).wait()
        rows = normed[:, :, cols(g)].reshape(micros * tokens, width)
        keyval_raw[...] += jnp.dot(
            rows, weight[cols(g), :], preferred_element_type=f32
        ).reshape(keyval_raw.shape)

    keyval_own[...] = keyval_raw[...].astype(bf16)
    pl.semaphore_wait(barrier, 2 + ranks - 1)
    for m in range(micros):
        for step in range(1, ranks):

            @pl.when(me < ranks - step)
            def _():
                keyval_copy(m, step).start()

    for m in range(micros):
        keyval_raw[m] = keyval_raw[m] / inverse[m]
        keyval[m, rank_rows(me), :] = keyval_own[m]
        owned[m, 0] = normed[m, :, share_cols(me)]
    for rank in range(1, ranks):

        @pl.when(me < rank)
        def _():
            keyval[:, rank * tokens : (rank + 1) * tokens, :] = jnp.zeros(
                (micros, tokens, keyval.shape[2]), bf16
            )

    for step in range(1, ranks):

        @pl.when(me >= ranks - step)
        def _():
            landed[:, :, step - 1] = jnp.zeros((micros, KVH, tokens, 2 * DH), bf16)

    @pl.when(sec < sections - 2)
    def _():
        for step in range(1, ranks):
            owned_copy(step).start()

    def forward(m, carry):
        for step in range(1, ranks):

            @pl.when(me >= step)
            def _():
                keyval_copy(m, step).wait_recv()

        @pl.loop(0, KVH)
        def _(g):
            queries = stacked(normed[m, :, cols(g)])
            scores = (
                lax.dot_general(
                    keyval[m, :, key_cols(g)], queries, NT_DIMS, preferred_element_type=f32
                )
                * SCALE
            )
            seen = jnp.concatenate([mask[m]] * (GROUP * tokens // mask.shape[2]), axis=1)
            scores = jnp.where(seen > 0.5, scores, -1e30)
            expo = jnp.exp(scores - jnp.max(scores, axis=0, keepdims=True))
            soft = expo / jnp.sum(expo, axis=0, keepdims=True)
            probs[m, g] = soft
            attn[m, g] = lax.dot_general(
                soft.astype(bf16), keyval[m, :, value_cols(g)], TN_DIMS, preferred_element_type=f32
            ).astype(bf16)

        return carry

    @pl.when(sec < sections - 1)
    def _():
        lax.fori_loop(0, micros, forward, 0)

    @pl.when(sec == sections - 1)
    def _():
        up[...] = top[...]

    def up_copy(m, g):
        return pltpu.make_async_remote_copy(
            src_ref=grads.at[m, :, cols(g)],
            dst_ref=up.at[m, :, cols(g)],
            send_sem=up_send.at[m, g],
            recv_sem=up_recv.at[m, g],
            device_id=(lax.rem(sec + sections - 1, sections), me),
            device_id_type=MESH,
        )

    def part_copy(m, g, slot, peer):
        return pltpu.make_async_remote_copy(
            src_ref=part.at[m, g, rank_rows(peer), :],
            dst_ref=landed.at[m, g, slot],
            send_sem=part_send.at[m, g, slot],
            recv_sem=part_recv.at[m, g, slot],
            device_id=(sec, peer),
            device_id_type=MESH,
        )

    def dkv_copy(m, step):
        return pltpu.make_async_remote_copy(
            src_ref=dkv_all.at[m, 0],
            dst_ref=dkv_all.at[m, step + 1],
            send_sem=dkv_send.at[m, step],
            recv_sem=dkv_recv.at[m, step],
            device_id=(sec, lax.rem(me + step + 1, ranks)),
            device_id_type=MESH,
        )

    def attend(m, g):
        @pl.when(sec < sections - 1)
        def _():
            up_copy(m, g).wait_recv()

        ups = stacked(up[m, :, cols(g)])
        queries = stacked(normed[m, :, cols(g)])
        keys = keyval[m, :, key_cols(g)]
        values = keyval[m, :, value_cols(g)]
        product = ups.astype(f32) * attn[m, g].astype(f32)
        high = product.astype(bf16)
        low = (product - high.astype(f32)).astype(bf16)
        delta = lax.dot_general(
            jnp.ones((16, 2 * DH), bf16),
            jnp.concatenate([high, low], axis=1),
            NT_DIMS,
            preferred_element_type=f32,
        )[:1]
        soft = probs[m, g]
        dprobs = lax.dot_general(values, ups, NT_DIMS, preferred_element_type=f32)
        dscores = (soft * (dprobs - delta) * SCALE).astype(bf16)
        part[m, g, :, DH:] = jnp.dot(
            soft.astype(bf16), ups, preferred_element_type=f32
        ).astype(bf16)
        part[m, g, :, :DH] = jnp.dot(dscores, queries, preferred_element_type=f32).astype(bf16)
        for step in range(1, ranks):

            @pl.when(me >= step)
            def _():
                part_copy(m, g, step - 1, lax.max(me - step, 0)).start()

        dq = lax.dot_general(dscores, keys, TN_DIMS, preferred_element_type=f32)
        dq = jnp.concatenate([dq[h * tokens : (h + 1) * tokens] for h in range(GROUP)], axis=1)
        scaled = gain[:, cols(g)] * dq
        mean[...] += jnp.sum(
            stream[m, :, cols(g)].astype(f32) * scaled, axis=-1, keepdims=True
        )
        base[:, cols(g)] = up[m, :, cols(g)].astype(f32) + inverse[m] * scaled

    def gather(m, g):
        for step in range(1, ranks):

            @pl.when(me < ranks - step)
            def _():
                part_copy(m, g, step - 1, lax.max(me - step, 0)).wait_recv()

        terms = part[m, g, rank_rows(me), :].astype(f32)
        for step in range(1, ranks):
            terms = terms + landed[m, g, step - 1].astype(f32)
        rounded = terms.astype(bf16)
        dkv_all[m, 0, :, key_cols(g)] = rounded[:, :DH]
        dkv_all[m, 0, :, value_cols(g)] = rounded[:, DH:]
        wide = rounded.astype(jnp.float32)
        return (
            wide[:, :DH] * keyval_raw[m, :, key_cols(g)]
            + wide[:, DH:] * keyval_raw[m, :, value_cols(g)]
        )

    def project(m, g, inv, pull):
        back = lax.dot_general(
            dkv_all[m, 0], weight[cols(g), :], NT_DIMS, preferred_element_type=jnp.float32
        )
        fresh = (
            base[:, cols(g)]
            + inv * (gain[:, cols(g)] * back)
            - stream[m, :, cols(g)].astype(f32) * pull
        )
        grads[m, :, cols(g)] = fresh.astype(jnp.bfloat16)

        @pl.when(sec > 0)
        def _():
            up_copy(m, g).start()

    def one_micro(m, carry):
        @pl.when(sec == sections - 1)
        def _():
            forward(m, carry)

        mean[...] = jnp.zeros_like(mean)
        for g in range(KVH):
            attend(m, g)
        pulls = gather(m, 0)
        for g in range(1, KVH):
            pulls = pulls + gather(m, g)
        for step in range(ranks - 1):
            dkv_copy(m, step).start()
        inv = inverse[m]
        mean_all = mean[...] + jnp.sum(pulls, axis=-1, keepdims=True)
        pull = inv * inv * inv * (mean_all * (1.0 / model))
        for g in range(KVH):
            project(m, g, inv, pull)
        return carry

    lax.fori_loop(0, micros, one_micro, 0)

    @pl.when(sec >= sections - 2)
    def _():
        for step in range(1, ranks):
            owned_copy(step).start()

    for step in range(1, ranks):
        owned_copy(step).wait_recv()
    for m in range(micros):
        for step in range(ranks - 1):
            dkv_copy(m, step).wait_recv()

    block = 256 if share % 256 == 0 else share

    @pl.loop(0, share // block)
    def _(i):
        here = pl.ds(pl.multiple_of(i * block, block), block)
        wgrad[here, :] = lax.dot_general(
            owned[:, :, :, here].reshape(micros * seq, block),
            dkv_all[...].reshape(micros * seq, wgrad.shape[1]),
            TN_DIMS,
            preferred_element_type=f32,
        ).astype(bf16)

    for step in range(1, ranks):
        owned_copy(step).wait_send()

        @pl.when(me < ranks - step)
        def _():
            for m in range(micros):
                keyval_copy(m, step).wait_send()

    for m in range(micros):
        for step in range(ranks - 1):
            dkv_copy(m, step).wait_send()

    def drain(m, carry):
        def drain_group(g):
            @pl.when(sec > 0)
            def _():
                up_copy(m, g).wait_send()

            for step in range(1, ranks):

                @pl.when(me >= step)
                def _():
                    part_copy(m, g, step - 1, lax.max(me - step, 0)).wait_send()

        pl.loop(0, KVH)(drain_group)
        return carry

    lax.fori_loop(0, micros, drain, 0)


def shards(stream_in, gain, kv_weight, pattern, top_grad):
    sections = lax.axis_size("section")
    ranks = lax.axis_size("dp")
    rank = lax.axis_index("dp")
    stream = stream_in[0]
    micros, tokens, model = stream.shape
    weight = kv_weight[0]
    kv_width = weight.shape[1] // 2
    seq = tokens * ranks

    tiles = seq // TILE
    query_pos = rank * tokens + jnp.arange(tokens)
    key_pos = jnp.arange(seq)
    seen = jnp.zeros((micros, tokens, seq), jnp.bool_)
    for row in range(tiles):
        for col in range(row + 1):
            pair = (query_pos[:, None] // TILE == row) & (key_pos[None, :] // TILE == col)
            seen = seen | (pair[None] & (pattern[:, row, col] > 0)[:, None, None])
    allowed = seen & (key_pos[None, :] <= query_pos[:, None])[None]

    mask = jnp.swapaxes(allowed, 1, 2).astype(jnp.float32)
    mask = jnp.tile(mask, (1, 1, max(1, DH // tokens)))

    vmem = pl.BlockSpec(memory_space=pltpu.VMEM)
    bf16, f32 = jnp.bfloat16, jnp.float32
    grads, wgrad = pl.pallas_call(
        functools.partial(relay, sections, ranks, micros, tokens),
        out_shape=(
            jax.ShapeDtypeStruct((micros, tokens, model), bf16),
            jax.ShapeDtypeStruct((model // ranks, 2 * kv_width), bf16),
        ),
        in_specs=[vmem, vmem, vmem, pl.BlockSpec(memory_space=pl.ANY), vmem],
        out_specs=(vmem, vmem),
        scratch_shapes=[
            pltpu.VMEM((model, 2 * kv_width), bf16),
            pltpu.VMEM((micros, tokens, model), bf16),
            pltpu.VMEM((micros, tokens, 1), f32),
            pltpu.VMEM((micros, tokens, 2 * kv_width), bf16),
            pltpu.VMEM((micros, seq, 2 * kv_width), bf16),
            pltpu.VMEM((micros, tokens, 2 * kv_width), f32),
            pltpu.VMEM((micros, KVH, seq, GROUP * tokens), f32),
            pltpu.VMEM((micros, KVH, GROUP * tokens, DH), bf16),
            pltpu.VMEM((micros, ranks, tokens, model // ranks), bf16),
            pltpu.VMEM((micros, tokens, model), bf16),
            pltpu.VMEM((micros, KVH, seq, 2 * DH), bf16),
            pltpu.VMEM((micros, KVH, ranks - 1, tokens, 2 * DH), bf16),
            pltpu.VMEM((tokens, model), f32),
            pltpu.VMEM((micros, ranks, tokens, 2 * kv_width), bf16),
            pltpu.VMEM((tokens, 1), f32),
            pltpu.SemaphoreType.DMA((KVH,)),
            pltpu.SemaphoreType.DMA((micros, ranks - 1)),
            pltpu.SemaphoreType.DMA((micros, ranks - 1)),
            pltpu.SemaphoreType.DMA((ranks - 1,)),
            pltpu.SemaphoreType.DMA((ranks - 1,)),
            pltpu.SemaphoreType.DMA((micros, KVH)),
            pltpu.SemaphoreType.DMA((micros, KVH)),
            pltpu.SemaphoreType.DMA((micros, KVH, ranks - 1)),
            pltpu.SemaphoreType.DMA((micros, KVH, ranks - 1)),
            pltpu.SemaphoreType.DMA((micros, ranks - 1)),
            pltpu.SemaphoreType.DMA((micros, ranks - 1)),
        ],
        compiler_params=pltpu.CompilerParams(
            collective_id=0, has_side_effects=True, vmem_limit_bytes=60 * 1024 * 1024
        ),
    )(top_grad, stream, gain.astype(f32), weight, mask)
    return grads[None], wgrad[None]


def solution(mesh):
    placed = (
        P("section", None, "dp", None),
        P("section", None),
        P("section", None, None),
        P(),
        P(None, "dp", None),
    )
    return jax.shard_map(
        shards,
        mesh=mesh,
        in_specs=placed,
        out_specs=(P("section", None, "dp", None), P("section", "dp", None)),
        check_vma=False,
    )
```
